32 devices in a mesh: section: 2 (over x), row: 4 (over z), col: 4 (over y, core).
Axes of the slice: x: 2, y: 2, z: 4, core: 2. Of those that a mesh axis runs over, the one named last changes fastest.
Arguments:
- grad_top: bfloat16 [1024, 12288], P(None, 'row'), may hold values from -6 to 6
- qkv_grad: bfloat16 [2, 1024, 18432], P('section', 'col', 'row'), may hold values from -1.5 to 1.5
- qkv_input: bfloat16 [2, 1024, 12288], P('section', None, 'row'), may hold values from -6 to 6
- qkv_weight: bfloat16 [2, 12288, 18432], P('section', 'row', 'col'), may hold values from -0.0546875 to 0.0546875
- attn_out: bfloat16 [2, 1024, 6144], P('section', None, 'col'), may hold values from -1.5 to 1.5
- out_weight: bfloat16 [2, 6144, 12288], P('section', 'col', 'row'), may hold values from -0.078125 to 0.078125
Outputs:
- qkv_weight_grad: bfloat16 [2, 12288, 18432], P('section', 'row', 'col')
- out_weight_grad: bfloat16 [2, 6144, 12288], P('section', 'col', 'row')
- attn_grad: bfloat16 [2, 1024, 6144], P('section', 'row', 'col')
- lower_grad: bfloat16 [2, 1024, 12288], P('section', 'col', 'row')
The draws below stay inside these ranges and needn't reach their ends.
All inputs are finite; a program needn't handle non-finite values.
Results may differ from the reference program's by a relative error of at most 0.014.
Values may be sent and summed in bfloat16 or wider, within the bound.
No kernel may reach another device: no remote copies, remote signals or barrier semaphores. Data moves between devices by JAX's collectives and lax.ppermute only.
A program may use at most 192 MiB of HBM per device.

```python
import jax
import jax.numpy as jnp
from jax import lax

D = 12288
QKV = 18432
DIN = 6144
TOKENS = 1024
SECTIONS = 2
N_ROW = 4
N_COL = 4


def spiked(entries, own_key, source, target, parts, factor):
    owner, partner = [(jnp.arange(entries.shape[axis_at]) // (entries.shape[axis_at] // parts)).reshape([-1 if axis == axis_at else 1 for axis in range(entries.ndim)]) for axis_at in (source, target)]
    chosen = jax.random.permutation(own_key, parts)[partner]
    strong = (owner == chosen) | (owner == (partner + parts // 2) % parts)
    return jnp.where(strong, factor * entries, entries)


def block_scale(rng, dims, split, smallest, high):
    def one(axis_at, parts):
        heights = jax.random.uniform(jax.random.fold_in(jax.random.fold_in(rng, 6), axis_at), (parts,), jnp.float32, smallest / len(split), high / len(split))
        return jnp.repeat(jnp.exp(heights), dims[axis_at] // parts).reshape((-1,) + (1,) * (len(dims) - axis_at - 1))

    level = one(*split[0])
    for cut in split[1:]:
        level = level * one(*cut)
    return level


def scatter_about(rng, extent, spread, bound, shards=(), held_as=jnp.bfloat16):
    gain = block_scale(rng, extent, shards, -0.22, 0.18) if shards else 1.0
    array = jax.random.normal(rng, extent, jnp.float32) * spread * gain
    return jnp.minimum(jnp.maximum(array, -bound), bound).astype(held_as)


def bell_draw_with(own_key, dims, width, reach, pieces, heavy, dtype=jnp.bfloat16):
    drawn = width * jax.random.normal(own_key, dims, jnp.float32)
    if pieces:
        drawn = drawn * block_scale(own_key, dims, pieces, -0.22, 0.18)
    return jnp.clip(spiked(drawn, jax.random.fold_in(own_key, 3), *heavy), -reach, reach).astype(dtype)


def setup_inputs(seed: int = 0) -> dict:
    key_of = jax.random.split(jax.random.key(seed), 7)
    return {
        "grad_top": bell_draw_with(key_of[0], (TOKENS, D), 1.0, 6.0, ((1, 4),), (1, 0, 4, 2.0)),
        "qkv_grad": bell_draw_with(key_of[1], (SECTIONS, TOKENS, QKV), 0.25, 1.5, ((0, 2), (1, 4), (2, 4)), (2, 1, 4, 2.0)),
        "qkv_input": scatter_about(key_of[2], (SECTIONS, TOKENS, D), 1.0, 6.0, ((0, 2), (2, 4))),
        "qkv_weight": scatter_about(key_of[3], (SECTIONS, D, QKV), D ** -0.5, 0.0546875, ((0, 2), (1, 4), (2, 4))),
        "attn_out": scatter_about(key_of[4], (SECTIONS, TOKENS, DIN), 0.25, 1.5, ((0, 2), (2, 4))),
        "out_weight": scatter_about(key_of[5], (SECTIONS, DIN, D), DIN ** -0.5, 0.078125, ((0, 2), (1, 4), (2, 4))),
    }


def rounded_sum(left_side, right_side, blocks):
    block_width = left_side.shape[1] // blocks
    summed = jnp.zeros((left_side.shape[0], right_side.shape[0]), jnp.float32)
    for block_index in range(blocks):
        first_col = block_index * block_width
        product = jnp.dot(left_side[:, first_col:first_col + block_width],
                          right_side[:, first_col:first_col + block_width].T,
                          preferred_element_type=jnp.float32)
        narrow = lax.optimization_barrier(product.astype(jnp.bfloat16))
        summed = summed + narrow.astype(jnp.float32)
    return summed


def reference(grad_top, qkv_grad, qkv_input, qkv_weight, attn_out, out_weight):
    upper_grad = grad_top
    qkv_grads = []
    out_grads = []
    attn_grads = []
    lower_grads = []
    for section_index in reversed(range(SECTIONS)):
        summed = rounded_sum(qkv_grad[section_index], qkv_weight[section_index], N_COL)
        lower_grad = (upper_grad.astype(jnp.float32) + summed).astype(jnp.bfloat16)
        qkv_grads.append(jnp.dot(qkv_input[section_index].T, qkv_grad[section_index],
                                 preferred_element_type=jnp.float32).astype(jnp.bfloat16))
        out_grads.append(jnp.dot(attn_out[section_index].T, upper_grad,
                                 preferred_element_type=jnp.float32).astype(jnp.bfloat16))
        attn_grads.append(rounded_sum(upper_grad, out_weight[section_index], N_ROW).astype(jnp.bfloat16))
        lower_grads.append(lower_grad)
        upper_grad = lower_grad
    return (jnp.stack(qkv_grads[::-1]), jnp.stack(out_grads[::-1]),
            jnp.stack(attn_grads[::-1]), jnp.stack(lower_grads[::-1]))
```

```python
import functools

import jax
import jax.numpy as jnp
from jax import lax
from jax.experimental import pallas as pl
from jax.experimental.pallas import tpu as pltpu
from jax.sharding import PartitionSpec as P

CHUNKS = (2, 1, 1)
PIECES = 3
VMEM = 60 * 2**20
BF16 = jnp.bfloat16
F32 = jnp.float32
EASE = 1
PARAMS = pltpu.CompilerParams(vmem_limit_bytes=VMEM)


def fitting(size, unit, most):
    return max(b for b in range(unit, most + 1, unit) if size % b == 0)


def cost(rows, depth, width):
    flops = 2 * rows * depth * width // EASE
    return pl.CostEstimate(flops=flops, bytes_accessed=flops // 1000, transcendentals=0)


def shape(dims, dtype):
    return jax.ShapeDtypeStruct(dims, dtype)


def swap(block, axis, bit):
    route = [(i, i ^ bit) for i in range(lax.axis_size(axis))]
    return lax.ppermute(block, axis, route)


def swap_below(block, bit):
    width = lax.axis_size("col")
    route = [
        (s * width + i, s * width + (i ^ bit))
        for s in range(lax.axis_size("section") - 1)
        for i in range(width)
    ]
    return lax.ppermute(block, ("section", "col"), route)


def shifted(block, axis, distance):
    devices = range(lax.axis_size(axis))
    route = [(i - distance, i) for i in devices if i - distance in devices]
    return lax.ppermute(block, axis, route)


def direct(block, step):
    n = lax.axis_size("row")
    route = [(j * n + (i ^ j ^ step), i * n + j) for i in range(n) for j in range(n)]
    return lax.ppermute(block, ("row", "col"), route)


def bits_down(n):
    return [1 << b for b in reversed(range(n.bit_length() - 1))]


def nt(left, right):
    return lax.dot_general(left, right, (((1,), (1,)), ((), ())), preferred_element_type=F32)


def turn_kernel(token, x_ref, out_ref):
    out_ref[...] = x_ref[...].T


def turned(token, x):
    n = token.shape[0]
    rows, cols = x.shape
    return pl.pallas_call(
        turn_kernel,
        out_shape=shape((cols, rows), x.dtype),
        grid_spec=pltpu.PrefetchScalarGridSpec(
            num_scalar_prefetch=1,
            grid=(n,),
            in_specs=[pl.BlockSpec((rows // n, cols), lambda d, token: (token[d], 0))],
            out_specs=pl.BlockSpec((cols, rows // n), lambda d, token: (0, d)),
        ),
        compiler_params=PARAMS,
        cost_estimate=cost(rows, cols, n),
        name="turn",
    )(token, x)


def halves(total, send_ref, keep_ref):
    for d in range(total.shape[0]):
        if d % 2:
            send_ref[d // 2] = total[d].astype(send_ref.dtype)
        else:
            keep_ref[d // 2] = total[d]


def terms_kernel(n, more, split, place, *refs):
    ins, weight_ref = refs[:n], refs[n]
    outs, held_ref = refs[n + 1 + more : -1], refs[-1]
    rows = ins[0].shape[0]

    @pl.when(pl.program_id(0) == 0)
    def _():
        for k in range(n):
            held_ref[pl.ds(pl.multiple_of(place[k] * rows, rows), rows), :] = ins[k][...]

    terms = nt(held_ref[...], weight_ref[...]).reshape(n, rows, -1)
    if more:
        terms = terms + refs[n + 1][...]
    if split:
        halves(terms, *outs)
    else:
        outs[0][...] = terms


def grad_terms(place, blocks, weight, piece, total=None, first=0, split=False):
    n = len(blocks)
    rows, depth = blocks[0].shape
    width = weight.shape[0]
    bn = fitting(width, 128, 512)
    more = total is not None
    chunk = first // rows
    keep = pl.BlockSpec((n // 2, rows, bn), lambda i, place: (0, 0, i))
    whole = pl.BlockSpec((n, rows, bn), lambda i, place: (0, 0, i))
    half = (n // 2, rows, width)
    sums = [shape(half, BF16), shape(half, F32)] if split else [shape((n, rows, width), F32)]
    return pl.pallas_call(
        functools.partial(terms_kernel, n, more, split),
        out_shape=sums + [shape((n * rows, depth), BF16)],
        grid_spec=pltpu.PrefetchScalarGridSpec(
            num_scalar_prefetch=1,
            grid=(width // bn,),
            in_specs=[pl.BlockSpec((rows, depth), lambda i, place: (0, 0))] * n
            + [pl.BlockSpec((bn, depth), lambda i, place: (i, piece))]
            + [pl.BlockSpec((n, rows, bn), lambda i, place: (0, chunk, i))] * more,
            out_specs=([keep, keep] if split else [whole])
            + [pl.BlockSpec((n * rows, depth), lambda i, place: (0, 0))],
        ),
        input_output_aliases={n + 2: 0} if more and not split else {},
        compiler_params=PARAMS,
        cost_estimate=cost(n * rows, depth, width),
        name="grad_terms",
    )(place, *blocks, weight, *[total] * more)


def attn_kernel(n, scalars, *refs):
    below, top = refs[:n], refs[n : 2 * n]
    weight_ref, send_ref, keep_ref, upper_ref, held_ref = refs[2 * n :]
    rows = below[0].shape[0]

    @pl.when(pl.program_id(0) == 0)
    def _():
        for d in range(n):
            upper = jnp.where(scalars[2 * n] == 1, top[d][0], below[d][...])
            upper_ref[d] = upper
            first = pl.multiple_of(scalars[n + d] * rows, rows)
            held_ref[pl.ds(first, rows), :] = upper

    terms = nt(held_ref[...], weight_ref[...])
    halves(terms.reshape(n, rows, -1), send_ref, keep_ref)


def attn_terms(scalars, below, grad_top, weight, first):
    n = len(below)
    rows, depth = below[0].shape
    width = weight.shape[0]
    bn = fitting(width, 128, 512)
    tops = grad_top.reshape(n, -1, depth)
    chunk = first // rows
    part = pl.BlockSpec((n // 2, rows, bn), lambda i, scalars: (0, 0, i))
    half = (n // 2, rows, width)
    return pl.pallas_call(
        functools.partial(attn_kernel, n),
        out_shape=[shape(half, BF16), shape(half, F32), shape((n, rows, depth), BF16)],
        grid_spec=pltpu.PrefetchScalarGridSpec(
            num_scalar_prefetch=1,
            grid=(width // bn,),
            in_specs=[pl.BlockSpec((rows, depth), lambda i, scalars: (0, 0))] * n
            + [
                pl.BlockSpec((1, rows, depth), lambda i, scalars, d=d: (scalars[d], chunk, 0))
                for d in range(n)
            ]
            + [pl.BlockSpec((bn, depth), lambda i, scalars: (i, 0))],
            out_specs=[
                part,
                part,
                pl.BlockSpec((n, rows, depth), lambda i, scalars: (0, 0, 0)),
            ],
            scratch_shapes=[pltpu.VMEM((n * rows, depth), BF16)],
        ),
        compiler_params=PARAMS,
        cost_estimate=cost(n * rows, depth, width),
        name="attn_terms",
    )(scalars, *below, *[tops] * n, weight)


def outer_kernel(order, scalars, left_ref, *refs):
    ins, out_ref = refs[: len(refs) - 1], refs[-1]
    right = [ins[a][first : first + rows] for a, first, rows in order]
    right = jnp.concatenate(right, axis=0) if len(right) > 1 else right[0]
    out_ref[...] = jnp.dot(left_ref[...], right, preferred_element_type=F32).astype(out_ref.dtype)


def outer_into_kernel(order, scalars, into_ref, left_ref, *refs):
    outer_kernel(order, scalars, left_ref, *refs)


def outer(scalars, left, rights, order, columns, first=0, into=None, part=(0, 1)):
    width = rights[0].shape[1] // part[1]
    bn = fitting(width, 128, 256)
    start = part[0] * width // bn
    offset = first // bn + start
    in_specs = [pl.BlockSpec(left.shape, lambda i, s: (0, 0))] + [
        pl.BlockSpec((a.shape[0], bn), lambda i, s: (0, i + start)) for a in rights
    ]
    kernel, args, aliases = outer_kernel, (left, *rights), {}
    if into is not None:
        in_specs = [pl.BlockSpec(memory_space=pl.ANY)] + in_specs
        kernel, args, aliases = outer_into_kernel, (into, *args), {1: 0}
    return pl.pallas_call(
        functools.partial(kernel, order),
        out_shape=shape((left.shape[0], columns), BF16),
        grid_spec=pltpu.PrefetchScalarGridSpec(
            num_scalar_prefetch=1,
            grid=(width // bn,),
            in_specs=in_specs,
            out_specs=pl.BlockSpec((left.shape[0], bn), lambda i, s: (0, i + offset)),
        ),
        input_output_aliases=aliases,
        compiler_params=PARAMS,
        cost_estimate=cost(*left.shape, width),
        name="outer",
    )(scalars, *args)


class Slots:
    def __init__(self):
        self.token = ()
        self.tasks = []

    def gate(self, block):
        return lax.optimization_barrier((block, self.token))[0]

    def run(self, choose):
        before, behind, tasks = [], [], []
        for task in self.tasks:
            step = next(task, None)
            if step is not None:
                before += step[0]
                behind += step[1]
                tasks.append(task)
        self.tasks = tasks
        token = self.token
        self.token = (*token, *before)
        for kernel in choose():
            made = kernel()
            behind.append(made)
            self.token = (made,)
        self.token = tuple(behind) or token


def summed(terms):
    total = terms[0].astype(F32)
    for term in terms[1:]:
        total = total + term.astype(F32)
    return total


def scatter(slots, send, keep, axis, short, done):
    terms = [[keep[p]] for p in range(keep.shape[0])]
    bit = 1
    before = []
    while True:
        got = swap(slots.gate(send), axis, bit)
        if bit > 1 or not short:
            yield before, [got]
            got = slots.gate(got)
        terms = [t + [got[p]] for p, t in enumerate(terms)]
        bit *= 2
        if bit == lax.axis_size(axis):
            break
        send = jnp.stack([summed(t) for t in terms[1::2]]).astype(BF16)
        before = [send]
        terms = terms[0::2]
    done += terms[0]


def per_device(grad_top, qkv_grad, qkv_input, qkv_weight, attn_out, out_weight):
    weight, own, out_tile = qkv_weight[0], qkv_grad[0], out_weight[0]
    n = lax.axis_size("row")
    row, col = lax.axis_index("row"), lax.axis_index("col")
    is_top = lax.axis_index("section") == lax.axis_size("section") - 1
    steps = jnp.arange(n, dtype=jnp.int32)
    token = col ^ steps
    share, columns = own.shape
    width = columns // PIECES
    unit = share // sum(CHUNKS)
    spans = [(sum(CHUNKS[:q]) * unit, c * unit) for q, c in enumerate(CHUNKS)]
    order = [(q, d * rows, rows) for d in range(n) for q, (_, rows) in enumerate(spans)]
    last_piece = PIECES - 1

    place = row ^ steps
    scalars = jnp.concatenate([token, row ^ col ^ steps, is_top.astype(jnp.int32)[None]])
    slots = Slots()
    have = {}

    def gather():
        for piece in range(PIECES):
            for q, (first, rows) in enumerate(spans if piece == last_piece else [(0, share)]):
                part = own[first : first + rows, piece * width : (piece + 1) * width]
                part = slots.gate(part)
                blocks = [direct(part, k) for k in range(n)]
                yield [], blocks
                have["blocks", piece, q] = blocks

    def relay(q):
        first, rows = spans[q]
        send, keep = have["terms", q]
        terms = []
        yield from scatter(slots, send, keep, "col", True, terms)
        down = summed(terms)
        top_own = lax.dynamic_slice_in_dim(grad_top, col * share + first, rows, 0)
        upper = top_own
        lower = (upper.astype(F32) + down).astype(BF16)
        for _ in range(lax.axis_size("section") - 1):
            handed = shifted(slots.gate(lower), "section", -1)
            yield [lower], [handed]
            handed = slots.gate(handed)
            upper = jnp.where(is_top, top_own, handed)
            lower = (upper.astype(F32) + down).astype(BF16)
        below = {0: handed}
        for bit in bits_down(n):
            got = {d | bit: swap_below(below[d], bit) for d in below}
            if bit > 1:
                yield [], list(got.values())
                got = {d: slots.gate(block) for d, block in got.items()}
                have["lower", q] = (slots.gate(upper).astype(F32) + down).astype(BF16)
            below.update(got)
        have["upper", q] = [below[d] for d in range(n)]

    def finish(q):
        send, keep = have["attn terms", q]
        terms = []
        yield from scatter(slots, send, keep, "row", False, terms)
        have["attn", q] = summed(terms).astype(BF16)

    def turn(name, array):
        def run():
            have[name] = turned(slots.gate(token), array)
            return have[name]

        return run

    def early_terms(piece):
        def run():
            have["early"], have["held", piece] = grad_terms(
                slots.gate(place), have["blocks", piece, 0], weight, piece, have.get("early")
            )
            return have["early"]

        return run

    def early_grad(piece):
        def run():
            have["grad"] = outer(
                slots.gate(place),
                have["inputs"],
                [have["held", piece]],
                [(0, 0, n * share)],
                columns,
                piece * width,
                have.get("grad"),
            )
            return have["grad"]

        return run

    def late_terms(q):
        def run():
            send, keep, have["late", q] = grad_terms(
                slots.gate(place),
                have["blocks", last_piece, q],
                weight,
                last_piece,
                have["early"],
                spans[q][0],
                True,
            )
            have["terms", q] = send, keep
            slots.tasks.append(relay(q))
            return send

        return run

    def late_grad(*part):
        def run():
            have["grad"] = outer(
                slots.gate(place),
                have["inputs"],
                [have["late", q] for q in range(len(spans))],
                order,
                columns,
                last_piece * width,
                have["grad"],
                part,
            )
            return have["grad"]

        return run

    def attn(q):
        def run():
            send, keep, upper = attn_terms(
                slots.gate(scalars), have["upper", q], grad_top, out_tile, spans[q][0]
            )
            have["attn terms", q] = send, keep
            have["uppers", q] = upper.reshape(-1, upper.shape[-1])
            slots.tasks.append(finish(q))
            return send

        return run

    def out_grad(*part):
        def run():
            have["out"] = outer(
                slots.gate(place),
                have["attn_out"],
                [have["uppers", q] for q in range(len(spans))],
                order,
                grad_top.shape[1],
                0,
                have.get("out"),
                part,
            )
            return have["out"]

        return run

    terms = [late_terms(q) for q in range(len(spans))]
    attns = [attn(q) for q in range(len(spans))]
    spare = [early_grad(last_piece - 1), late_grad(0, 2), late_grad(1, 2)]
    outs = [out_grad(0, 2), out_grad(1, 2)]

    def late():
        if terms:
            return [terms.pop(0)]
        if attns and ("upper", len(spans) - len(attns)) in have:
            more = len(attns) < len(spans) and len(attns) > 1
            return [attns.pop(0)] + [spare.pop(0) for _ in spare[: int(more)]]
        if spare and attns:
            return [spare.pop(0)]
        return [kernel for few in (spare, outs) for kernel in [few.pop(0) for _ in few[:1]]]

    slots.tasks.append(gather())
    slots.run(lambda: [turn("inputs", qkv_input[0]), turn("attn_out", attn_out[0])])
    for piece in range(last_piece):
        both = piece < last_piece - 1
        slots.run(lambda: [early_terms(piece)] + [early_grad(piece)] * both)
    while slots.tasks or terms or attns or spare or outs:
        slots.run(late)

    every = range(len(spans))
    return (
        have["grad"][None],
        have["out"][None],
        jnp.concatenate([have["attn", q] for q in every], axis=0)[None],
        jnp.concatenate([have["lower", q] for q in every], axis=0)[None],
    )


def solution(mesh):
    return jax.shard_map(
        per_device,
        mesh=mesh,
        in_specs=(
            P(None, "row"),
            P("section", "col", "row"),
            P("section", None, "row"),
            P("section", "row", "col"),
            P("section", None, "col"),
            P("section", "col", "row"),
        ),
        out_specs=(
            P("section", "row", "col"),
            P("section", "col", "row"),
            P("section", "row", "col"),
            P("section", "col", "row"),
        ),
        check_vma=False,
    )
```

```python
import functools

import jax
import jax.numpy as jnp
from jax import lax
from jax.experimental import pallas as pl
from jax.experimental.pallas import tpu as pltpu
from jax.sharding import PartitionSpec as P

CHUNKS = (1, 1)
PIECES = (1, 1)
VMEM = 60 * 2**20
BF16 = jnp.bfloat16
F32 = jnp.float32
EASE = 1
PARAMS = pltpu.CompilerParams(vmem_limit_bytes=VMEM)


def fitting(size, unit, most):
    return max(b for b in range(unit, most + 1, unit) if size % b == 0)


def cost(rows, depth, width):
    flops = 2 * rows * depth * width // EASE
    return pl.CostEstimate(flops=flops, bytes_accessed=flops // 1000, transcendentals=0)


def shape(dims, dtype):
    return jax.ShapeDtypeStruct(dims, dtype)


def swap(block, axis, bit):
    route = [(i, i ^ bit) for i in range(lax.axis_size(axis))]
    return lax.ppermute(block, axis, route)


def swap_below(block, bit):
    width = lax.axis_size("col")
    route = [
        (s * width + i, s * width + (i ^ bit))
        for s in range(lax.axis_size("section") - 1)
        for i in range(width)
    ]
    return lax.ppermute(block, ("section", "col"), route)


def shifted(block, axis, distance):
    devices = range(lax.axis_size(axis))
    route = [(i - distance, i) for i in devices if i - distance in devices]
    return lax.ppermute(block, axis, route)


def direct(block, step):
    n = lax.axis_size("row")
    route = [(j * n + (i ^ j ^ step), i * n + j) for i in range(n) for j in range(n)]
    return lax.ppermute(block, ("row", "col"), route)


def bits_down(n):
    return [1 << b for b in reversed(range(n.bit_length() - 1))]


def nt(left, right):
    return lax.dot_general(left, right, (((1,), (1,)), ((), ())), preferred_element_type=F32)


def turn_kernel(token, x_ref, out_ref):
    out_ref[...] = x_ref[...].T


def turned(token, x):
    n = token.shape[0]
    rows, cols = x.shape
    return pl.pallas_call(
        turn_kernel,
        out_shape=shape((cols, rows), x.dtype),
        grid_spec=pltpu.PrefetchScalarGridSpec(
            num_scalar_prefetch=1,
            grid=(n,),
            in_specs=[pl.BlockSpec((rows // n, cols), lambda d, token: (token[d], 0))],
            out_specs=pl.BlockSpec((cols, rows // n), lambda d, token: (0, d)),
        ),
        compiler_params=PARAMS,
        cost_estimate=cost(rows, cols, n),
        name="turn",
    )(token, x)


def halves(total, send_ref, keep_ref):
    for d in range(total.shape[0]):
        if d % 2:
            send_ref[d // 2] = total[d].astype(send_ref.dtype)
        else:
            keep_ref[d // 2] = total[d]


def terms_kernel(n, more, split, place, *refs):
    ins, weight_ref = refs[:n], refs[n]
    outs, held_ref = refs[n + 1 + more : -1], refs[-1]
    rows = ins[0].shape[0]

    @pl.when(pl.program_id(0) == 0)
    def _():
        for k in range(n):
            held_ref[pl.ds(pl.multiple_of(place[k] * rows, rows), rows), :] = ins[k][...]

    terms = nt(held_ref[...], weight_ref[...]).reshape(n, rows, -1)
    if more:
        terms = terms + refs[n + 1][...]
    if split:
        halves(terms, *outs)
    else:
        outs[0][...] = terms


def grad_terms(place, blocks, weight, piece, total=None, first=0, split=False):
    n = len(blocks)
    rows, depth = blocks[0].shape
    width = weight.shape[0]
    bn = fitting(width, 128, 512)
    more = total is not None
    chunk = first // rows
    piece = piece[0] // piece[1]
    keep = pl.BlockSpec((n // 2, rows, bn), lambda i, place: (0, 0, i))
    whole = pl.BlockSpec((n, rows, bn), lambda i, place: (0, 0, i))
    half = (n // 2, rows, width)
    sums = [shape(half, BF16), shape(half, F32)] if split else [shape((n, rows, width), F32)]
    return pl.pallas_call(
        functools.partial(terms_kernel, n, more, split),
        out_shape=sums + [shape((n * rows, depth), BF16)],
        grid_spec=pltpu.PrefetchScalarGridSpec(
            num_scalar_prefetch=1,
            grid=(width // bn,),
            in_specs=[pl.BlockSpec((rows, depth), lambda i, place: (0, 0))] * n
            + [pl.BlockSpec((bn, depth), lambda i, place: (i, piece))]
            + [pl.BlockSpec((n, rows, bn), lambda i, place: (0, chunk, i))] * more,
            out_specs=([keep, keep] if split else [whole])
            + [pl.BlockSpec((n * rows, depth), lambda i, place: (0, 0))],
        ),
        input_output_aliases={n + 2: 0} if more and not split else {},
        compiler_params=PARAMS,
        cost_estimate=cost(n * rows, depth, width),
        name="grad_terms",
    )(place, *blocks, weight, *[total] * more)


def attn_kernel(n, scalars, *refs):
    below, top = refs[:n], refs[n : 2 * n]
    weight_ref, send_ref, keep_ref, upper_ref, held_ref = refs[2 * n :]
    rows = below[0].shape[0]

    @pl.when(pl.program_id(0) == 0)
    def _():
        for d in range(n):
            upper = jnp.where(scalars[2 * n] == 1, top[d][0], below[d][...])
            upper_ref[d] = upper
            first = pl.multiple_of(scalars[n + d] * rows, rows)
            held_ref[pl.ds(first, rows), :] = upper

    terms = nt(held_ref[...], weight_ref[...])
    halves(terms.reshape(n, rows, -1), send_ref, keep_ref)


def attn_terms(scalars, below, grad_top, weight, first):
    n = len(below)
    rows, depth = below[0].shape
    width = weight.shape[0]
    bn = fitting(width, 128, 512)
    tops = grad_top.reshape(n, -1, depth)
    chunk = first // rows
    part = pl.BlockSpec((n // 2, rows, bn), lambda i, scalars: (0, 0, i))
    half = (n // 2, rows, width)
    return pl.pallas_call(
        functools.partial(attn_kernel, n),
        out_shape=[shape(half, BF16), shape(half, F32), shape((n, rows, depth), BF16)],
        grid_spec=pltpu.PrefetchScalarGridSpec(
            num_scalar_prefetch=1,
            grid=(width // bn,),
            in_specs=[pl.BlockSpec((rows, depth), lambda i, scalars: (0, 0))] * n
            + [
                pl.BlockSpec((1, rows, depth), lambda i, scalars, d=d: (scalars[d], chunk, 0))
                for d in range(n)
            ]
            + [pl.BlockSpec((bn, depth), lambda i, scalars: (i, 0))],
            out_specs=[
                part,
                part,
                pl.BlockSpec((n, rows, depth), lambda i, scalars: (0, 0, 0)),
            ],
            scratch_shapes=[pltpu.VMEM((n * rows, depth), BF16)],
        ),
        compiler_params=PARAMS,
        cost_estimate=cost(n * rows, depth, width),
        name="attn_terms",
    )(scalars, *below, *[tops] * n, weight)


def outer_kernel(order, scalars, left_ref, *refs):
    ins, out_ref = refs[: len(refs) - 1], refs[-1]
    right = [ins[a][first : first + rows] for a, first, rows in order]
    right = jnp.concatenate(right, axis=0) if len(right) > 1 else right[0]
    out_ref[...] = jnp.dot(left_ref[...], right, preferred_element_type=F32).astype(out_ref.dtype)


def outer_into_kernel(order, scalars, into_ref, left_ref, *refs):
    outer_kernel(order, scalars, left_ref, *refs)


def outer(scalars, left, rights, order, columns, first=0, into=None, part=(0, 1)):
    width = rights[0].shape[1] // part[1]
    bn = fitting(width, 128 if width % 256 else 256, 512)
    start = part[0] * width // bn
    offset = first // bn + start
    in_specs = [pl.BlockSpec(left.shape, lambda i, s: (0, 0))] + [
        pl.BlockSpec((a.shape[0], bn), lambda i, s: (0, i + start)) for a in rights
    ]
    kernel, args, aliases = outer_kernel, (left, *rights), {}
    if into is not None:
        in_specs = [pl.BlockSpec(memory_space=pl.ANY)] + in_specs
        kernel, args, aliases = outer_into_kernel, (into, *args), {1: 0}
    return pl.pallas_call(
        functools.partial(kernel, order),
        out_shape=shape((left.shape[0], columns), BF16),
        grid_spec=pltpu.PrefetchScalarGridSpec(
            num_scalar_prefetch=1,
            grid=(width // bn,),
            in_specs=in_specs,
            out_specs=pl.BlockSpec((left.shape[0], bn), lambda i, s: (0, i + offset)),
        ),
        input_output_aliases=aliases,
        compiler_params=PARAMS,
        cost_estimate=cost(*left.shape, width),
        name="outer",
    )(scalars, *args)


class Slots:
    def __init__(self):
        self.token = ()
        self.tasks = []

    def gate(self, block):
        return lax.optimization_barrier((block, self.token))[0]

    def run(self, choose):
        before, behind, tasks = [], [], []
        for task in self.tasks:
            step = next(task, None)
            if step is not None:
                before += step[0]
                behind += step[1]
                tasks.append(task)
        self.tasks = tasks
        token = self.token
        self.token = (*token, *before)
        count = len(behind)
        for kernel in choose():
            made = kernel()
            self.token = (made,)
            behind = behind[:count] + [made]
        self.token = tuple(behind) or token


def summed(terms):
    total = terms[0].astype(F32)
    for term in terms[1:]:
        total = total + term.astype(F32)
    return total


def scatter(slots, send, keep, axis, short, done):
    terms = [[keep[p]] for p in range(keep.shape[0])]
    bit = 1
    before = []
    while True:
        got = swap(slots.gate(send), axis, bit)
        if bit > 1 or not short:
            yield before, [got]
            got = slots.gate(got)
        terms = [t + [got[p]] for p, t in enumerate(terms)]
        bit *= 2
        if bit == lax.axis_size(axis):
            break
        send = jnp.stack([summed(t) for t in terms[1::2]]).astype(BF16)
        before = [send]
        terms = terms[0::2]
    done += terms[0]


def per_device(grad_top, qkv_grad, qkv_input, qkv_weight, attn_out, out_weight):
    weight, own, out_tile = qkv_weight[0], qkv_grad[0], out_weight[0]
    n = lax.axis_size("row")
    row, col = lax.axis_index("row"), lax.axis_index("col")
    is_top = lax.axis_index("section") == lax.axis_size("section") - 1
    steps = jnp.arange(n, dtype=jnp.int32)
    token = col ^ steps
    share, columns = own.shape
    step = columns // sum(PIECES)
    pieces = [(sum(PIECES[:p]) * step, w * step) for p, w in enumerate(PIECES)]
    unit = share // sum(CHUNKS)
    spans = [(sum(CHUNKS[:q]) * unit, c * unit) for q, c in enumerate(CHUNKS)]
    order = [(q, d * rows, rows) for d in range(n) for q, (_, rows) in enumerate(spans)]
    last_piece = len(PIECES) - 1

    place = row ^ steps
    scalars = jnp.concatenate([token, row ^ col ^ steps, is_top.astype(jnp.int32)[None]])
    slots = Slots()
    have = {}

    def gather():
        for piece, (start, width) in enumerate(pieces):
            for q, (first, rows) in enumerate(spans if piece == last_piece else [(0, share)]):
                part = own[first : first + rows, start : start + width]
                part = slots.gate(part)
                blocks = [direct(part, k) for k in range(n)]
                yield [], blocks
                have["blocks", piece, q] = blocks

    def relay(q):
        first, rows = spans[q]
        send, keep = have["terms", q]
        terms = []
        yield from scatter(slots, send, keep, "col", True, terms)
        down = summed(terms)
        top_own = lax.dynamic_slice_in_dim(grad_top, col * share + first, rows, 0)
        upper = top_own
        lower = (upper.astype(F32) + down).astype(BF16)
        for _ in range(lax.axis_size("section") - 1):
            handed = shifted(slots.gate(lower), "section", -1)
            yield [lower], [handed]
            handed = slots.gate(handed)
            upper = jnp.where(is_top, top_own, handed)
            lower = (upper.astype(F32) + down).astype(BF16)
        below = {0: handed}
        for bit in bits_down(n):
            got = {d | bit: swap_below(below[d], bit) for d in below}
            if bit > 1:
                yield [], list(got.values())
                got = {d: slots.gate(block) for d, block in got.items()}
                have["lower", q] = (slots.gate(upper).astype(F32) + down).astype(BF16)
            below.update(got)
        have["upper", q] = [below[d] for d in range(n)]

    def finish(q):
        send, keep = have["attn terms", q]
        terms = []
        yield from scatter(slots, send, keep, "row", False, terms)
        have["attn", q] = summed(terms).astype(BF16)

    def turn(name, array):
        def run():
            have[name] = turned(slots.gate(token), array)
            return have[name]

        return run

    def early_terms(piece):
        def run():
            have["early"], have["held", piece] = grad_terms(
                slots.gate(place), have["blocks", piece, 0], weight, pieces[piece], have.get("early")
            )
            return have["early"]

        return run

    def early_grad(piece):
        def run():
            have["grad"] = outer(
                slots.gate(place),
                have["inputs"],
                [have["held", piece]],
                [(0, 0, n * share)],
                columns,
                pieces[piece][0],
                have.get("grad"),
            )
            return have["grad"]

        return run

    def late_terms(q):
        def run():
            send, keep, have["late", q] = grad_terms(
                slots.gate(place),
                have["blocks", last_piece, q],
                weight,
                pieces[last_piece],
                have["early"],
                spans[q][0],
                True,
            )
            have["terms", q] = send, keep
            slots.tasks.append(relay(q))
            return send

        return run

    def late_grad(*part):
        def run():
            have["grad"] = outer(
                slots.gate(place),
                have["inputs"],
                [have["late", q] for q in range(len(spans))],
                order,
                columns,
                pieces[last_piece][0],
                have["grad"],
                part,
            )
            return have["grad"]

        return run

    def attn(q):
        def run():
            send, keep, upper = attn_terms(
                slots.gate(scalars), have["upper", q], grad_top, out_tile, spans[q][0]
            )
            have["attn terms", q] = send, keep
            have["uppers", q] = upper.reshape(-1, upper.shape[-1])
            slots.tasks.append(finish(q))
            return send

        return run

    def out_grad(*part):
        def run():
            have["out"] = outer(
                slots.gate(place),
                have["attn_out"],
                [have["uppers", q] for q in range(len(spans))],
                order,
                grad_top.shape[1],
                0,
                have.get("out"),
                part,
            )
            return have["out"]

        return run

    terms = [late_terms(q) for q in range(len(spans))]
    attns = [attn(q) for q in range(len(spans))]
    spare = [early_grad(last_piece - 1), *[late_grad(part, 3) for part in range(3)]]
    outs = [out_grad(0, 1)]

    def late():
        if terms:
            return [terms.pop(0)] + [spare.pop(0) for _ in spare[:1] if len(spare) == 4]
        if attns and ("upper", len(spans) - len(attns)) in have:
            more = len(attns) < len(spans) and len(attns) > 1
            return [attns.pop(0)] + [spare.pop(0) for _ in spare[: int(more)]]
        if spare and attns:
            return [spare.pop(0) for _ in spare[: max(1, len(spare) - 1)]]
        if attns:
            return []
        final = spare + outs
        spare.clear()
        outs.clear()
        return final

    slots.tasks.append(gather())
    slots.run(lambda: [turn("inputs", qkv_input[0]), turn("attn_out", attn_out[0])])
    for piece in range(last_piece):
        both = piece < last_piece - 1
        slots.run(lambda: [early_terms(piece)] + [early_grad(piece)] * both)
    while slots.tasks or terms or attns or spare or outs:
        slots.run(late)

    every = range(len(spans))
    return (
        have["grad"][None],
        have["out"][None],
        jnp.concatenate([have["attn", q] for q in every], axis=0)[None],
        jnp.concatenate([have["lower", q] for q in every], axis=0)[None],
    )


def solution(mesh):
    return jax.shard_map(
        per_device,
        mesh=mesh,
        in_specs=(
            P(None, "row"),
            P("section", "col", "row"),
            P("section", None, "row"),
            P("section", "row", "col"),
            P("section", None, "col"),
            P("section", "col", "row"),
        ),
        out_specs=(
            P("section", "row", "col"),
            P("section", "col", "row"),
            P("section", "row", "col"),
            P("section", "col", "row"),
        ),
        check_vma=False,
    )
```

```python
import functools

import jax
import jax.numpy as jnp
from jax import lax
from jax.experimental import pallas as pl
from jax.experimental.pallas import tpu as pltpu
from jax.sharding import PartitionSpec as P

CHUNKS = (1, 1)
PIECES = (1, 1)
VMEM = 60 * 2**20
BF16 = jnp.bfloat16
F32 = jnp.float32
EASE = 1
PARAMS = pltpu.CompilerParams(vmem_limit_bytes=VMEM)


def fitting(size, unit, most):
    return max(b for b in range(unit, most + 1, unit) if size % b == 0)


def cost(rows, depth, width):
    flops = 2 * rows * depth * width // EASE
    return pl.CostEstimate(flops=flops, bytes_accessed=flops // 1000, transcendentals=0)


def shape(dims, dtype):
    return jax.ShapeDtypeStruct(dims, dtype)


def swap(block, axis, bit):
    route = [(i, i ^ bit) for i in range(lax.axis_size(axis))]
    return lax.ppermute(block, axis, route)


def swap_below(block, bit):
    width = lax.axis_size("col")
    route = [
        (s * width + i, s * width + (i ^ bit))
        for s in range(lax.axis_size("section") - 1)
        for i in range(width)
    ]
    return lax.ppermute(block, ("section", "col"), route)


def shifted(block, axis, distance):
    devices = range(lax.axis_size(axis))
    route = [(i - distance, i) for i in devices if i - distance in devices]
    return lax.ppermute(block, axis, route)


def direct(block, step):
    n = lax.axis_size("row")
    route = [(j * n + (i ^ j ^ step), i * n + j) for i in range(n) for j in range(n)]
    return lax.ppermute(block, ("row", "col"), route)


def bits_down(n):
    return [1 << b for b in reversed(range(n.bit_length() - 1))]


def nt(left, right):
    return lax.dot_general(left, right, (((1,), (1,)), ((), ())), preferred_element_type=F32)


def turn_kernel(token, x_ref, out_ref):
    out_ref[...] = x_ref[...].T


def turned(token, x):
    n = token.shape[0]
    rows, cols = x.shape
    return pl.pallas_call(
        turn_kernel,
        out_shape=shape((cols, rows), x.dtype),
        grid_spec=pltpu.PrefetchScalarGridSpec(
            num_scalar_prefetch=1,
            grid=(n,),
            in_specs=[pl.BlockSpec((rows // n, cols), lambda d, token: (token[d], 0))],
            out_specs=pl.BlockSpec((cols, rows // n), lambda d, token: (0, d)),
        ),
        compiler_params=PARAMS,
        cost_estimate=cost(rows, cols, n),
        name="turn",
    )(token, x)


def halves(total, send_ref, keep_ref):
    for d in range(total.shape[0]):
        if d % 2:
            send_ref[d // 2] = total[d].astype(send_ref.dtype)
        else:
            keep_ref[d // 2] = total[d]


def terms_kernel(n, more, split, place, *refs):
    ins, weight_ref = refs[:n], refs[n]
    outs, held_ref = refs[n + 1 + more : -1], refs[-1]
    rows = ins[0].shape[0]

    @pl.when(pl.program_id(0) == 0)
    def _():
        for k in range(n):
            held_ref[pl.ds(pl.multiple_of(place[k] * rows, rows), rows), :] = ins[k][...]

    terms = nt(held_ref[...], weight_ref[...]).reshape(n, rows, -1)
    if more:
        terms = terms + refs[n + 1][...]
    if split:
        halves(terms, *outs)
    else:
        outs[0][...] = terms


def grad_terms(place, blocks, weight, piece, total=None, first=0, split=False):
    n = len(blocks)
    rows, depth = blocks[0].shape
    width = weight.shape[0]
    bn = fitting(width, 128, 512)
    more = total is not None
    chunk = first // rows
    piece = piece[0] // piece[1]
    keep = pl.BlockSpec((n // 2, rows, bn), lambda i, place: (0, 0, i))
    whole = pl.BlockSpec((n, rows, bn), lambda i, place: (0, 0, i))
    half = (n // 2, rows, width)
    sums = [shape(half, BF16), shape(half, F32)] if split else [shape((n, rows, width), F32)]
    return pl.pallas_call(
        functools.partial(terms_kernel, n, more, split),
        out_shape=sums + [shape((n * rows, depth), BF16)],
        grid_spec=pltpu.PrefetchScalarGridSpec(
            num_scalar_prefetch=1,
            grid=(width // bn,),
            in_specs=[pl.BlockSpec((rows, depth), lambda i, place: (0, 0))] * n
            + [pl.BlockSpec((bn, depth), lambda i, place: (i, piece))]
            + [pl.BlockSpec((n, rows, bn), lambda i, place: (0, chunk, i))] * more,
            out_specs=([keep, keep] if split else [whole])
            + [pl.BlockSpec((n * rows, depth), lambda i, place: (0, 0))],
        ),
        input_output_aliases={n + 2: 0} if more and not split else {},
        compiler_params=PARAMS,
        cost_estimate=cost(n * rows, depth, width),
        name="grad_terms",
    )(place, *blocks, weight, *[total] * more)


def attn_kernel(n, scalars, *refs):
    below, top = refs[:n], refs[n : 2 * n]
    weight_ref, send_ref, keep_ref, upper_ref, held_ref = refs[2 * n :]
    rows = below[0].shape[0]

    @pl.when(pl.program_id(0) == 0)
    def _():
        for d in range(n):
            upper = jnp.where(scalars[2 * n] == 1, top[d][0], below[d][...])
            upper_ref[d] = upper
            first = pl.multiple_of(scalars[n + d] * rows, rows)
            held_ref[pl.ds(first, rows), :] = upper

    terms = nt(held_ref[...], weight_ref[...])
    halves(terms.reshape(n, rows, -1), send_ref, keep_ref)


def attn_terms(scalars, below, grad_top, weight, first):
    n = len(below)
    rows, depth = below[0].shape
    width = weight.shape[0]
    bn = fitting(width, 128, 512)
    tops = grad_top.reshape(n, -1, depth)
    chunk = first // rows
    part = pl.BlockSpec((n // 2, rows, bn), lambda i, scalars: (0, 0, i))
    half = (n // 2, rows, width)
    return pl.pallas_call(
        functools.partial(attn_kernel, n),
        out_shape=[shape(half, BF16), shape(half, F32), shape((n, rows, depth), BF16)],
        grid_spec=pltpu.PrefetchScalarGridSpec(
            num_scalar_prefetch=1,
            grid=(width // bn,),
            in_specs=[pl.BlockSpec((rows, depth), lambda i, scalars: (0, 0))] * n
            + [
                pl.BlockSpec((1, rows, depth), lambda i, scalars, d=d: (scalars[d], chunk, 0))
                for d in range(n)
            ]
            + [pl.BlockSpec((bn, depth), lambda i, scalars: (i, 0))],
            out_specs=[
                part,
                part,
                pl.BlockSpec((n, rows, depth), lambda i, scalars: (0, 0, 0)),
            ],
            scratch_shapes=[pltpu.VMEM((n * rows, depth), BF16)],
        ),
        compiler_params=PARAMS,
        cost_estimate=cost(n * rows, depth, width),
        name="attn_terms",
    )(scalars, *below, *[tops] * n, weight)


def outer_kernel(order, scalars, left_ref, *refs):
    ins, out_ref = refs[: len(refs) - 1], refs[-1]
    right = [ins[a][first : first + rows] for a, first, rows in order]
    right = jnp.concatenate(right, axis=0) if len(right) > 1 else right[0]
    out_ref[...] = jnp.dot(left_ref[...], right, preferred_element_type=F32).astype(out_ref.dtype)


def outer_into_kernel(order, scalars, into_ref, left_ref, *refs):
    outer_kernel(order, scalars, left_ref, *refs)


def outer(scalars, left, rights, order, columns, first=0, into=None, part=(0, 1)):
    width = rights[0].shape[1] // part[1]
    bn = fitting(width, 128 if width % 256 else 256, 512)
    start = part[0] * width // bn
    offset = first // bn + start
    in_specs = [pl.BlockSpec(left.shape, lambda i, s: (0, 0))] + [
        pl.BlockSpec((a.shape[0], bn), lambda i, s: (0, i + start)) for a in rights
    ]
    kernel, args, aliases = outer_kernel, (left, *rights), {}
    if into is not None:
        in_specs = [pl.BlockSpec(memory_space=pl.ANY)] + in_specs
        kernel, args, aliases = outer_into_kernel, (into, *args), {1: 0}
    return pl.pallas_call(
        functools.partial(kernel, order),
        out_shape=shape((left.shape[0], columns), BF16),
        grid_spec=pltpu.PrefetchScalarGridSpec(
            num_scalar_prefetch=1,
            grid=(width // bn,),
            in_specs=in_specs,
            out_specs=pl.BlockSpec((left.shape[0], bn), lambda i, s: (0, i + offset)),
        ),
        input_output_aliases=aliases,
        compiler_params=PARAMS,
        cost_estimate=cost(*left.shape, width),
        name="outer",
    )(scalars, *args)


class Slots:
    def __init__(self):
        self.token = ()
        self.tasks = []

    def gate(self, block):
        return lax.optimization_barrier((block, self.token))[0]

    def run(self, choose):
        before, behind, tasks = [], [], []
        for task in self.tasks:
            step = next(task, None)
            if step is not None:
                before += step[0]
                behind += step[1]
                tasks.append(task)
        self.tasks = tasks
        token = self.token
        self.token = (*token, *before)
        count = len(behind)
        for kernel in choose():
            made = kernel()
            self.token = (made,)
            behind = behind[:count] + [made]
        self.token = tuple(behind) or token


def summed(terms):
    total = terms[0].astype(F32)
    for term in terms[1:]:
        total = total + term.astype(F32)
    return total


def scatter(slots, send, keep, axis, short, done):
    terms = [[keep[p]] for p in range(keep.shape[0])]
    bit = 1
    before = []
    while True:
        got = swap(slots.gate(send), axis, bit)
        if bit > 1 or not short:
            yield before, [got]
            got = slots.gate(got)
        terms = [t + [got[p]] for p, t in enumerate(terms)]
        bit *= 2
        if bit == lax.axis_size(axis):
            break
        send = jnp.stack([summed(t) for t in terms[1::2]]).astype(BF16)
        before = [send]
        terms = terms[0::2]
    done += terms[0]


def per_device(grad_top, qkv_grad, qkv_input, qkv_weight, attn_out, out_weight):
    weight, own, out_tile = qkv_weight[0], qkv_grad[0], out_weight[0]
    n = lax.axis_size("row")
    row, col = lax.axis_index("row"), lax.axis_index("col")
    is_top = lax.axis_index("section") == lax.axis_size("section") - 1
    steps = jnp.arange(n, dtype=jnp.int32)
    token = col ^ steps
    share, columns = own.shape
    step = columns // sum(PIECES)
    pieces = [(sum(PIECES[:p]) * step, w * step) for p, w in enumerate(PIECES)]
    unit = share // sum(CHUNKS)
    spans = [(sum(CHUNKS[:q]) * unit, c * unit) for q, c in enumerate(CHUNKS)]
    order = [(q, d * rows, rows) for d in range(n) for q, (_, rows) in enumerate(spans)]
    last_piece = len(PIECES) - 1

    place = row ^ steps
    scalars = jnp.concatenate([token, row ^ col ^ steps, is_top.astype(jnp.int32)[None]])
    slots = Slots()
    have = {}

    def gather():
        for piece, (start, width) in enumerate(pieces):
            for q, (first, rows) in enumerate(spans if piece == last_piece else [(0, share)]):
                part = own[first : first + rows, start : start + width]
                part = slots.gate(part)
                blocks = [direct(part, k) for k in range(n)]
                yield [], blocks
                have["blocks", piece, q] = blocks

    def relay(q):
        first, rows = spans[q]
        send, keep = have["terms", q]
        terms = []
        yield from scatter(slots, send, keep, "col", True, terms)
        down = summed(terms)
        top_own = lax.dynamic_slice_in_dim(grad_top, col * share + first, rows, 0)
        upper = top_own
        lower = (upper.astype(F32) + down).astype(BF16)
        for _ in range(lax.axis_size("section") - 1):
            handed = shifted(slots.gate(lower), "section", -1)
            yield [lower], [handed]
            handed = slots.gate(handed)
            upper = jnp.where(is_top, top_own, handed)
            lower = (upper.astype(F32) + down).astype(BF16)
        below = {0: handed}
        for bit in bits_down(n):
            got = {d | bit: swap_below(below[d], bit) for d in below}
            if bit > 1:
                yield [], list(got.values())
                got = {d: slots.gate(block) for d, block in got.items()}
                have["lower", q] = upper, down
            below.update(got)
        have["upper", q] = [below[d] for d in range(n)]

    def finish(q):
        send, keep = have["attn terms", q]
        terms = []
        yield from scatter(slots, send, keep, "row", False, terms)
        have["attn", q] = summed(terms).astype(BF16)

    def turn(name, array):
        def run():
            have[name] = turned(slots.gate(token), array)
            return have[name]

        return run

    def early_terms(piece):
        def run():
            have["early"], have["held", piece] = grad_terms(
                slots.gate(place), have["blocks", piece, 0], weight, pieces[piece], have.get("early")
            )
            return have["early"]

        return run

    def early_grad(piece):
        def run():
            have["grad"] = outer(
                slots.gate(place),
                have["inputs"],
                [have["held", piece]],
                [(0, 0, n * share)],
                columns,
                pieces[piece][0],
                have.get("grad"),
            )
            return have["grad"]

        return run

    def late_terms(q):
        def run():
            send, keep, have["late", q] = grad_terms(
                slots.gate(place),
                have["blocks", last_piece, q],
                weight,
                pieces[last_piece],
                have["early"],
                spans[q][0],
                True,
            )
            have["terms", q] = send, keep
            slots.tasks.append(relay(q))
            return send

        return run

    def late_grad(*part):
        def run():
            have["grad"] = outer(
                slots.gate(place),
                have["inputs"],
                [have["late", q] for q in range(len(spans))],
                order,
                columns,
                pieces[last_piece][0],
                have["grad"],
                part,
            )
            return have["grad"]

        return run

    def attn(q):
        def run():
            send, keep, upper = attn_terms(
                slots.gate(scalars), have["upper", q], grad_top, out_tile, spans[q][0]
            )
            have["attn terms", q] = send, keep
            have["uppers", q] = upper.reshape(-1, upper.shape[-1])
            slots.tasks.append(finish(q))
            return send

        return run

    def out_grad(*part):
        def run():
            have["out"] = outer(
                slots.gate(place),
                have["attn_out"],
                [have["uppers", q] for q in range(len(spans))],
                order,
                grad_top.shape[1],
                0,
                have.get("out"),
                part,
            )
            return have["out"]

        return run

    terms = [late_terms(q) for q in range(len(spans))]
    attns = [attn(q) for q in range(len(spans))]
    spare = [early_grad(last_piece - 1), *[late_grad(part, 3) for part in range(3)]]
    outs = [out_grad(0, 1)]

    def late():
        if terms:
            return [terms.pop(0)] + [spare.pop(0) for _ in spare[:1] if len(spare) == 4]
        if attns and ("upper", len(spans) - len(attns)) in have:
            more = len(attns) < len(spans) and len(attns) > 1
            return [attns.pop(0)] + [spare.pop(0) for _ in spare[: int(more)]]
        if spare and attns:
            return [spare.pop(0) for _ in spare[: max(1, len(spare) - 1)]]
        if attns:
            return []
        if not spare and not outs:
            return [ends.pop()] if ends else []
        final = spare + outs
        spare.clear()
        outs.clear()
        return final

    def lowers():
        parts = [have["lower", q] for q in range(len(spans))]
        parts = [(slots.gate(upper).astype(F32) + down).astype(BF16) for upper, down in parts]
        have["lowers"] = jnp.concatenate(parts, axis=0)
        return have["lowers"]

    ends = [lowers]
    slots.tasks.append(gather())
    slots.run(lambda: [turn("inputs", qkv_input[0]), turn("attn_out", attn_out[0])])
    for piece in range(last_piece):
        both = piece < last_piece - 1
        slots.run(lambda: [early_terms(piece)] + [early_grad(piece)] * both)
    while slots.tasks or terms or attns or spare or outs or ends:
        slots.run(late)

    every = range(len(spans))
    return (
        have["grad"][None],
        have["out"][None],
        jnp.concatenate([have["attn", q] for q in every], axis=0)[None],
        have["lowers"][None],
    )


def solution(mesh):
    return jax.shard_map(
        per_device,
        mesh=mesh,
        in_specs=(
            P(None, "row"),
            P("section", "col", "row"),
            P("section", None, "row"),
            P("section", "row", "col"),
            P("section", None, "col"),
            P("section", "col", "row"),
        ),
        out_specs=(
            P("section", "row", "col"),
            P("section", "col", "row"),
            P("section", "row", "col"),
            P("section", "col", "row"),
        ),
        check_vma=False,
    )
```
